512 devices in a mesh: seq: 64 (over y, x, core), head: 8 (over z).
Axes of the slice: x: 4, y: 8, z: 8, core: 2. Of those that a mesh axis runs over, the one named last changes fastest.
Arguments:
- query_act: bfloat16 [32768, 4096], P('seq', 'head'), may hold values from -6 to 6
- key_act: bfloat16 [32768, 4096], P('seq', 'head'), may hold values from -6 to 6
- value_act: bfloat16 [32768, 4096], P('seq', 'head'), may hold values from -16 to 16
- upstream: bfloat16 [32768, 4096], P('seq', 'head'), may hold values from -6 to 6
- norm_gain: float32 [4096], P('head'), may hold values from 0.1 to 1.9
Outputs:
- grad_query: bfloat16 [32768, 4096], P('seq', 'head')
- grad_key: bfloat16 [32768, 4096], P('seq', 'head')
- grad_value: bfloat16 [32768, 4096], P('seq', 'head')
The draws below stay inside these ranges and needn't reach their ends.
All inputs are finite; a program needn't handle non-finite values.
Results may differ from the reference program's by a relative error of at most 0.0058.
Values sent between devices are 32-bit elements; how exact they have to be, the bound alone decides.
A program may use at most 64 MiB of HBM per device.

```python
import jax
import jax.numpy as jnp
from jax import lax

HEADS = 32
HD = 128
CH = 128
SEQ = 32768
FEATURES = 4096


def draw_value_act(key, part):
    head_index = jnp.arange(HEADS * HD) // HD
    position = head_index.astype(jnp.float32) / max(HEADS - 1, 1)
    factor = 3.0 ** position
    sample = jax.random.normal(key, (SEQ, HEADS * HD), jnp.float32)
    return jnp.clip(sample * factor[None, :], -16.0, 16.0).astype(jnp.bfloat16)


def shard_levels(key, dims, cuts, low, largest):
    gain, own = 1.0, jax.random.fold_in(key, 6)
    for axis_at, shards_of in cuts:
        draws = jnp.exp(jax.random.uniform(jax.random.fold_in(own, axis_at), (shards_of,), jnp.float32, low / len(cuts), largest / len(cuts)))
        gain = gain * jnp.repeat(draws, dims[axis_at] // shards_of).reshape([-1 if axis == axis_at else 1 for axis in range(len(dims))])
    return gain


def bell_draw(stream_key, extent, scale, reach, cuts=(), held_as=jnp.bfloat16):
    entries = jax.random.normal(stream_key, extent, jnp.float32) * scale
    if len(cuts) > 0:
        entries = shard_levels(stream_key, extent, cuts, -0.22, 0.18) * entries
    return jnp.clip(entries, min=-reach, max=reach).astype(held_as)


def setup_inputs(seed: int = 0) -> dict:
    keys = jax.random.split(jax.random.key(seed), 6)
    return {
        "query_act": bell_draw(keys[0], (SEQ, FEATURES), 1.0, 6.0, ((0, 64), (1, 8))),
        "key_act": bell_draw(keys[1], (SEQ, FEATURES), 1.0, 6.0, ((0, 64), (1, 8))),
        "value_act": draw_value_act(jax.random.fold_in(keys[5], 71), 0),
        "upstream": bell_draw(keys[3], (SEQ, FEATURES), 1.0, 6.0, ((0, 64), (1, 8))),
        "norm_gain": jnp.clip(1.0 + 0.18 * jax.random.normal(keys[4], (FEATURES,), jnp.float32), 0.1, 1.9),
    }


def causal_mask():
    rows = lax.broadcasted_iota(jnp.int32, (CH, CH), 0)
    columns = lax.broadcasted_iota(jnp.int32, (CH, CH), 1)
    return (columns <= rows).astype(jnp.float32)

def rounded(values):
    return lax.optimization_barrier(values.astype(jnp.bfloat16)).astype(jnp.float32)

def exclusive_prefix(states):
    zeros = jnp.zeros_like(states[:1])
    return jnp.concatenate([zeros, jnp.cumsum(states, 0)[:-1]], 0)

def exclusive_suffix(states):
    after = jnp.cumsum(states[::-1], 0)[::-1]
    return jnp.concatenate([after[1:], jnp.zeros_like(states[:1])], 0)

def split_heads(matrix):
    return matrix.reshape(SEQ // CH, CH, HEADS, HD).transpose(2, 0, 1, 3)

def join_heads(blocks):
    return blocks.transpose(1, 2, 0, 3).reshape(SEQ, HEADS * HD)

def head_forward(operands):
    query_blk = operands[0].astype(jnp.float32)
    key_blk = operands[1].astype(jnp.float32)
    value_blk = operands[2].astype(jnp.float32)
    kv_state = rounded(exclusive_prefix(jnp.einsum('cti,ctj->cij', key_blk, value_blk)))
    fwd_scores = rounded(jnp.einsum('cti,csi->cts', query_blk, key_blk) * causal_mask())
    return jnp.einsum('cts,csj->ctj', fwd_scores, value_blk) + jnp.einsum('cti,cij->ctj', query_blk, kv_state)

def head_backward(operands):
    query_blk = operands[0].astype(jnp.float32)
    key_blk = operands[1].astype(jnp.float32)
    value_blk = operands[2].astype(jnp.float32)
    grad_blk = operands[3].astype(jnp.float32)
    causal = causal_mask()
    kv_state = rounded(exclusive_prefix(jnp.einsum('cti,ctj->cij', key_blk, value_blk)))
    fwd_scores = rounded(jnp.einsum('cti,csi->cts', query_blk, key_blk) * causal)
    back_scores = rounded(jnp.einsum('ctj,csj->cts', grad_blk, value_blk) * causal)
    qd_state = rounded(exclusive_suffix(jnp.einsum('cti,ctj->cij', query_blk, grad_blk)))
    grad_q = jnp.einsum('cts,csi->cti', back_scores, key_blk) + jnp.einsum('ctj,cij->cti', grad_blk, kv_state)
    grad_k = jnp.einsum('cts,cti->csi', back_scores, query_blk) + jnp.einsum('csj,cij->csi', value_blk, qd_state)
    grad_v = jnp.einsum('cts,ctj->csj', fwd_scores, grad_blk) + jnp.einsum('csi,cij->csj', key_blk, qd_state)
    return (grad_q.astype(jnp.bfloat16), grad_k.astype(jnp.bfloat16), grad_v.astype(jnp.bfloat16))

def reference(query_act, key_act, value_act, upstream, norm_gain):
    query_heads = split_heads(query_act)
    key_heads = split_heads(key_act)
    value_heads = split_heads(value_act)
    attention = lax.map(head_forward, (query_heads, key_heads, value_heads))
    guided = norm_gain.reshape(HEADS, 1, 1, HD) * split_heads(upstream).astype(jnp.float32)
    inverse = lax.rsqrt(lax.optimization_barrier(jnp.mean(attention * attention, axis=(0, 3))) + 1e-06)[None, :, :, None]
    cross = lax.optimization_barrier(jnp.mean(guided * attention, axis=(0, 3)))[None, :, :, None]
    grad_attn = lax.optimization_barrier((inverse * guided - inverse ** 3 * cross * attention).astype(jnp.bfloat16))
    grad_q, grad_k, grad_v = lax.map(head_backward, (query_heads, key_heads, value_heads, grad_attn))
    return (join_heads(grad_q), join_heads(grad_k), join_heads(grad_v))
```

```python
import functools

import jax
import jax.numpy as jnp
from jax import lax
from jax.experimental import pallas as pl
from jax.experimental.pallas import tpu as pltpu
from jax.sharding import PartitionSpec as P

HD = 128
CH = 128
NX = 4
MESH = pl.DeviceIdType.MESH
F32 = jnp.float32
BF16 = jnp.bfloat16


def mm(a, b, ca, cb):
    return lax.dot_general(a, b, (((ca,), (cb,)), ((), ())), preferred_element_type=F32)


def kernel(
    ny, nz, width,
    q_ref, k_ref, v_ref, g_ref, gain_ref, dq_ref, dk_ref, dv_ref,
    loc, tot, fs, att, kvs, gvp, ga,
    cbuf, chip, xin, ysrc, ybuf, xret, rbuf, csrc, cret, zsrc, zbuf,
    c_ss, c_rs, x_ss, x_rs, y_ss, y_rs, r_ss, r_rs, e_ss, e_rs, z_ss, z_rs,
):
    groups = q_ref.shape[0] // CH
    heads = q_ref.shape[1] // HD
    half = heads * HD // 2
    part = half // NX
    me = lax.axis_index("seq")
    z = lax.axis_index("head")
    core = lax.rem(me, 2)
    x = lax.rem(me // 2, NX)
    y = me // (2 * NX)
    other = me + 1 - 2 * core

    def at_x(j):
        return {"seq": (y * NX + j) * 2 + core}

    def at_y(j):
        return {"seq": (j * NX + x) * 2 + core}

    barrier = pltpu.get_barrier_semaphore()
    pl.semaphore_signal(barrier, inc=1, device_id={"seq": other}, device_id_type=MESH)
    for d in range(1, NX):
        pl.semaphore_signal(barrier, inc=1, device_id=at_x(lax.rem(x + d, NX)), device_id_type=MESH)
    for d in range(1, ny):
        pl.semaphore_signal(barrier, inc=1, device_id=at_y(lax.rem(y + d, ny)), device_id_type=MESH)
    for d in range(1, nz):
        pl.semaphore_signal(barrier, inc=1, device_id={"head": lax.rem(z + d, nz)}, device_id_type=MESH)

    started = []

    def send(src, dst, ss, rs, to):
        copy = pltpu.make_async_remote_copy(
            src_ref=src, dst_ref=dst, send_sem=ss, recv_sem=rs, device_id=to, device_id_type=MESH
        )
        copy.start()
        started.append(copy)
        return copy

    def blk(ref, c, h):
        return ref[c * CH:(c + 1) * CH, h * HD:(h + 1) * HD]

    row = lax.broadcasted_iota(jnp.int32, (CH, CH), 0)
    col = lax.broadcasted_iota(jnp.int32, (CH, CH), 1)
    causal = col <= row

    def scan(s, reverse, beside):
        mine = pl.ds(pl.multiple_of(core * half, 128), half)
        theirs = pl.ds(pl.multiple_of((1 - core) * half, 128), half)
        c1 = send(tot.at[s, theirs], cbuf.at[s], c_ss.at[s], c_rs.at[s], {"seq": other})
        beside[0]()
        c1.wait_recv()
        chip[s] = tot[s, mine] + cbuf[s]
        xs = []
        for d in range(1, NX):
            j = lax.rem(x + d, NX)
            xs.append(send(
                chip.at[s, pl.ds(pl.multiple_of(j * part, 8), part)], xin.at[s, x],
                x_ss.at[s, d - 1], x_rs.at[s, d - 1], at_x(j),
            ))
        xin[s, x] = chip[s, pl.ds(pl.multiple_of(x * part, 8), part)]
        beside[1]()
        for c in xs:
            c.wait_recv()
        total = xin[s, 0]
        for j in range(1, NX):
            total = total + xin[s, j]
        ysrc[s] = total
        ys = []
        for d in range(1, ny):
            ys.append(send(
                ysrc.at[s], ybuf.at[s, y], y_ss.at[s, d - 1], y_rs.at[s, d - 1],
                at_y(lax.rem(y + d, ny)),
            ))
        ybuf[s, y] = total
        beside[2]()
        for c in ys:
            c.wait_recv()
        run = jnp.zeros((part, HD), F32)
        for j in range(ny):
            reached = j > y if reverse else j < y
            run = run + jnp.where(reached, ybuf[s, j], 0.0)
        order = range(NX - 1, -1, -1) if reverse else range(NX)
        for j in order:
            xret[s, j] = run
            run = run + xin[s, j]
        rs = []
        for d in range(1, NX):
            j = lax.rem(x + d, NX)
            rs.append(send(
                xret.at[s, j], rbuf.at[s, pl.ds(pl.multiple_of(x * part, 8), part)],
                r_ss.at[s, d - 1], r_rs.at[s, d - 1], at_x(j),
            ))
        rbuf[s, pl.ds(pl.multiple_of(x * part, 8), part)] = xret[s, x]
        beside[3]()
        for c in rs:
            c.wait_recv()
        last = core == (0 if reverse else 1)
        csrc[s] = rbuf[s] + jnp.where(last, 0.0, tot[s, mine])
        e = send(csrc.at[s], cret.at[s, mine], e_ss.at[s], e_rs.at[s], {"seq": other})
        cret[s, mine] = rbuf[s] + jnp.where(last, cbuf[s], 0.0)
        e.wait_recv()

    def kv_part(h):
        run = None
        for c in range(groups):
            group = mm(blk(k_ref, c, h), blk(v_ref, c, h), 0, 0)
            if c > 0:
                loc[c, h] = run
            run = group if c == 0 else run + group
        tot[0, h * HD:(h + 1) * HD] = run

    def fwd_part(h):
        for c in range(groups):
            scores = mm(blk(q_ref, c, h), blk(k_ref, c, h), 1, 1)
            scores = jnp.where(causal, scores, 0.0).astype(BF16)
            fs[c, h] = scores
            att[c, h] = mm(scores, blk(v_ref, c, h), 1, 0)

    def guided(c, h):
        return gain_ref[:, h * HD:(h + 1) * HD] * blk(g_ref, c, h).astype(F32)

    for h in range(heads):
        kv_part(h)
    pl.semaphore_wait(barrier, 1 + (NX - 1) + (ny - 1) + (nz - 1))

    def nothing():
        pass

    def fwd_some(lo, hi):
        def go():
            for h in range(lo, hi):
                fwd_part(h)
        return go

    scan(0, False, [nothing, fwd_some(0, heads // 2), fwd_some(heads // 2, heads), nothing])

    for c in range(groups):
        squares = jnp.zeros((CH, HD), F32)
        crossed = jnp.zeros((CH, HD), F32)
        for h in range(heads):
            state = cret[0, h * HD:(h + 1) * HD]
            if c > 0:
                state = state + loc[c, h]
            state = state.astype(BF16)
            kvs[c, h] = state
            a = att[c, h] + mm(blk(q_ref, c, h), state, 1, 0)
            att[c, h] = a
            squares = squares + a * a
            crossed = crossed + guided(c, h) * a
        zsrc[c:c + 1, :] = jnp.sum(squares.T, 0, keepdims=True)
        zsrc[groups + c:groups + c + 1, :] = jnp.sum(crossed.T, 0, keepdims=True)
    zs = []
    for d in range(1, nz):
        zs.append(send(
            zsrc, zbuf.at[z], z_ss.at[d - 1], z_rs.at[d - 1], {"head": lax.rem(z + d, nz)}
        ))
    zbuf[z] = zsrc[...]
    for c in zs:
        c.wait_recv()
    sums = zbuf[0]
    for j in range(1, nz):
        sums = sums + zbuf[j]
    sums = sums * (1.0 / width)
    inverse = lax.rsqrt(sums[:groups] + 1e-06)
    second = inverse * inverse * inverse * sums[groups:]
    run = [None] * heads
    for c in range(groups - 1, -1, -1):
        inv = jnp.broadcast_to(inverse[c:c + 1], (CH, CH)).T
        sec = jnp.broadcast_to(second[c:c + 1], (CH, CH)).T
        for h in range(heads):
            grad = (inv * guided(c, h) - sec * att[c, h]).astype(BF16)
            ga[c, h] = grad
            group = mm(blk(q_ref, c, h), grad, 0, 0)
            if c < groups - 1:
                loc[c, h] = run[h]
            run[h] = group if c == groups - 1 else run[h] + group
    for h in range(heads):
        tot[1, h * HD:(h + 1) * HD] = run[h]

    def back_part(h):
        for c in range(groups):
            grad = ga[c, h]
            back = mm(grad, blk(v_ref, c, h), 1, 1)
            back = jnp.where(causal, back, 0.0).astype(BF16)
            gq = mm(back, blk(k_ref, c, h), 1, 0) + mm(grad, kvs[c, h], 1, 1)
            dq_ref[c * CH:(c + 1) * CH, h * HD:(h + 1) * HD] = gq.astype(BF16)
            att[c, h] = mm(back, blk(q_ref, c, h), 0, 0)
            gvp[c, h] = mm(fs[c, h], grad, 0, 0)

    def back_some(lo, hi):
        def go():
            for h in range(lo, hi):
                back_part(h)
        return go

    scan(1, True, [nothing, back_some(0, heads // 2), back_some(heads // 2, heads), nothing])

    for h in range(heads):
        for c in range(groups):
            state = cret[1, h * HD:(h + 1) * HD]
            if c < groups - 1:
                state = state + loc[c, h]
            state = state.astype(BF16)
            gk = att[c, h] + mm(blk(v_ref, c, h), state, 1, 1)
            dk_ref[c * CH:(c + 1) * CH, h * HD:(h + 1) * HD] = gk.astype(BF16)
            gv = gvp[c, h] + mm(blk(k_ref, c, h), state, 1, 0)
            dv_ref[c * CH:(c + 1) * CH, h * HD:(h + 1) * HD] = gv.astype(BF16)
    for copy in started:
        copy.wait_send()


def solution(mesh):
    ny = mesh.shape["seq"] // (2 * NX)
    nz = mesh.shape["head"]

    def on_device(query, key, value, upstream, gain):
        rows, columns = query.shape
        groups, heads = rows // CH, columns // HD
        half = columns // 2
        part = half // NX
        vmem = pl.BlockSpec(memory_space=pltpu.VMEM)
        out = jax.ShapeDtypeStruct((rows, columns), BF16)
        dma = pltpu.SemaphoreType.DMA
        blocks = (groups, heads, CH, HD)
        return pl.pallas_call(
            functools.partial(kernel, ny, nz, columns * nz),
            name="linear_attention_backward",
            out_shape=(out, out, out),
            in_specs=[vmem] * 5,
            out_specs=(vmem, vmem, vmem),
            scratch_shapes=[
                pltpu.VMEM(blocks, F32),
                pltpu.VMEM((2, columns, HD), F32),
                pltpu.VMEM(blocks, BF16),
                pltpu.VMEM(blocks, F32),
                pltpu.VMEM(blocks, BF16),
                pltpu.VMEM(blocks, F32),
                pltpu.VMEM(blocks, BF16),
                pltpu.VMEM((2, half, HD), F32),
                pltpu.VMEM((2, half, HD), F32),
                pltpu.VMEM((2, NX, part, HD), F32),
                pltpu.VMEM((2, part, HD), F32),
                pltpu.VMEM((2, ny, part, HD), F32),
                pltpu.VMEM((2, NX, part, HD), F32),
                pltpu.VMEM((2, half, HD), F32),
                pltpu.VMEM((2, half, HD), F32),
                pltpu.VMEM((2, columns, HD), F32),
                pltpu.VMEM((2 * groups, CH), F32),
                pltpu.VMEM((nz, 2 * groups, CH), F32),
                dma((2,)), dma((2,)),
                dma((2, NX - 1)), dma((2, NX - 1)),
                dma((2, ny - 1)), dma((2, ny - 1)),
                dma((2, NX - 1)), dma((2, NX - 1)),
                dma((2,)), dma((2,)),
                dma((nz - 1,)), dma((nz - 1,)),
            ],
            compiler_params=pltpu.CompilerParams(
                collective_id=0, has_side_effects=True, vmem_limit_bytes=40 * 1024 * 1024
            ),
        )(query, key, value, upstream, gain.reshape(1, columns))

    spec = P("seq", "head")
    return jax.shard_map(
        on_device, mesh=mesh, in_specs=(spec, spec, spec, spec, P("head")),
        out_specs=(spec, spec, spec), check_vma=False,
    )
```

```python
import functools

import jax
import jax.numpy as jnp
from jax import lax
from jax.experimental import pallas as pl
from jax.experimental.pallas import tpu as pltpu
from jax.sharding import PartitionSpec as P

HD = 128
CH = 128
NX = 4
TOGETHER = 1
MESH = pl.DeviceIdType.MESH
F32 = jnp.float32
BF16 = jnp.bfloat16


def mm(a, b, ca, cb):
    return lax.dot_general(a, b, (((ca,), (cb,)), ((), ())), preferred_element_type=F32)


def far_first(n):
    return sorted(range(1, n), key=lambda d: -min(d, n - d))


def kernel(
    ny, nz, width,
    q_hbm, k_hbm, v_hbm, g_hbm, gain_hbm, dq_hbm, dk_hbm, dv_hbm,
    dq_ref, dk_ref, dv_ref, q_ref, k_ref, v_ref, g_ref, gain_ref,
    loc, tot, fs, att, kvs, gvp, ga,
    cbuf, chip, xin, ysrc, ybuf, xret, rbuf, csrc, cret, zsrc, zbuf,
    out_s, in_s, gain_s, c_ss, c_rs, x_ss, x_rs, y_ss, y_rs, r_ss, r_rs, e_ss, e_rs, z_ss, z_rs,
):
    groups = q_ref.shape[0] // CH
    heads = q_ref.shape[1] // HD
    chunks = heads // TOGETHER
    half = TOGETHER * HD // 2
    part = half // NX
    me = lax.axis_index("seq")
    z = lax.axis_index("head")
    core = lax.rem(me, 2)
    x = lax.rem(me // 2, NX)
    y = me // (2 * NX)
    other = me + 1 - 2 * core

    def load(n, src, dst, h):
        cols = slice(h * HD, (h + 1) * HD)
        copy = pltpu.make_async_copy(src.at[:, cols], dst.at[:, cols], in_s.at[n, h])
        copy.start()
        return copy

    loads = {}
    for h in range(heads):
        loads[1, h] = load(1, k_hbm, k_ref, h)
        loads[2, h] = load(2, v_hbm, v_ref, h)
    for h in range(heads):
        loads[0, h] = load(0, q_hbm, q_ref, h)
    for h in range(heads):
        loads[3, h] = load(3, g_hbm, g_ref, h)
    gain_copy = pltpu.make_async_copy(gain_hbm, gain_ref, gain_s)
    gain_copy.start()

    stored = []

    def store(n, src, dst, h):
        cols = slice(h * HD, (h + 1) * HD)
        copy = pltpu.make_async_copy(src.at[:, cols], dst.at[:, cols], out_s.at[n, h])
        copy.start()
        stored.append(copy)

    def at_x(j):
        return {"seq": (y * NX + j) * 2 + core}

    def at_y(j):
        return {"seq": (j * NX + x) * 2 + core}

    barrier = pltpu.get_barrier_semaphore()
    for d in range(1, ny):
        pl.semaphore_signal(barrier, inc=1, device_id=at_y(lax.rem(y + d, ny)), device_id_type=MESH)
    for d in range(1, nz):
        pl.semaphore_signal(barrier, inc=1, device_id={"head": lax.rem(z + d, nz)}, device_id_type=MESH)
    for d in range(1, NX):
        pl.semaphore_signal(barrier, inc=1, device_id=at_x(lax.rem(x + d, NX)), device_id_type=MESH)
    pl.semaphore_signal(barrier, inc=1, device_id={"seq": other}, device_id_type=MESH)

    def send(src, dst, ss, rs, to):
        copy = pltpu.make_async_remote_copy(
            src_ref=src, dst_ref=dst, send_sem=ss, recv_sem=rs, device_id=to, device_id_type=MESH
        )
        copy.start()

    def blk(ref, c, h):
        return ref[c * CH:(c + 1) * CH, h * HD:(h + 1) * HD]

    row = lax.broadcasted_iota(jnp.int32, (CH, CH), 0)
    col = lax.broadcasted_iota(jnp.int32, (CH, CH), 1)
    causal = col <= row
    mine = pl.ds(pl.multiple_of(core * half, half), half)
    theirs = pl.ds(pl.multiple_of((1 - core) * half, half), half)

    def xpart(j):
        return pl.ds(pl.multiple_of(j * part, part), part)

    def arrived(like, sem):
        pltpu.make_async_copy(like, like, sem).wait()

    def spot(h):
        return h // TOGETHER, slice(h % TOGETHER * HD, (h % TOGETHER + 1) * HD)

    def sent(s):
        arrived(cbuf.at[s], c_ss.at[s])
        arrived(xin.at[s, :, pl.ds(0, NX - 1)], x_ss.at[s])
        arrived(ybuf.at[s, :, pl.ds(0, ny - 1)], y_ss.at[s])
        arrived(xret.at[s, :, pl.ds(0, NX - 1)], r_ss.at[s])
        arrived(cbuf.at[s], e_ss.at[s])

    def scan(s, reverse, produce, beside_x, beside_y, consume):
        last = core == (0 if reverse else 1)
        for k in range(chunks):
            produce(k)
            if s == 0 and k == 0:
                pl.semaphore_wait(barrier, 1 + (NX - 1) + (ny - 1) + (nz - 1))
            send(
                tot.at[s, k, theirs], cbuf.at[s, k], c_ss.at[s], c_rs.at[s, k], {"seq": other}
            )
        for k in range(chunks):
            arrived(cbuf.at[s, k], c_rs.at[s, k])
            chip[s, k] = tot[s, k, mine] + cbuf[s, k]
            for d in far_first(NX):
                j = lax.rem(x + d, NX)
                send(
                    chip.at[s, k, xpart(j)], xin.at[s, k, x],
                    x_ss.at[s], x_rs.at[s, k], at_x(j),
                )
            xin[s, k, x] = chip[s, k, xpart(x)]
        beside_x()
        for k in range(chunks):
            arrived(xin.at[s, k, pl.ds(0, NX - 1)], x_rs.at[s, k])
            total = xin[s, k, 0]
            for j in range(1, NX):
                total = total + xin[s, k, j]
            ysrc[s, k] = total
            for d in far_first(ny):
                send(
                    ysrc.at[s, k], ybuf.at[s, k, y], y_ss.at[s], y_rs.at[s, k],
                    at_y(lax.rem(y + d, ny)),
                )
            ybuf[s, k, y] = total
        beside_y()
        for k in range(chunks):
            arrived(ybuf.at[s, k, pl.ds(0, ny - 1)], y_rs.at[s, k])
            run = jnp.zeros((part, HD), F32)
            for j in range(ny):
                reached = j > y if reverse else j < y
                run = run + jnp.where(reached, ybuf[s, k, j], 0.0)
            order = range(NX - 1, -1, -1) if reverse else range(NX)
            for j in order:
                xret[s, k, j] = run
                run = run + xin[s, k, j]
            for d in far_first(NX):
                send(
                    xret.at[s, k, lax.rem(x + d, NX)], rbuf.at[s, k, xpart(x)],
                    r_ss.at[s], r_rs.at[s, k], at_x(lax.rem(x + d, NX)),
                )
            rbuf[s, k, xpart(x)] = xret[s, k, x]
        for k in range(chunks + 1):
            if k < chunks:
                arrived(rbuf.at[s, k, pl.ds(0, (NX - 1) * part)], r_rs.at[s, k])
                csrc[s, k] = rbuf[s, k] + jnp.where(last, 0.0, tot[s, k, mine])
                send(
                    csrc.at[s, k], cret.at[s, k, mine], e_ss.at[s], e_rs.at[s, k], {"seq": other}
                )
                cret[s, k, mine] = rbuf[s, k] + jnp.where(last, cbuf[s, k], 0.0)
            if k > 0:
                arrived(cret.at[s, k - 1, pl.ds(0, half)], e_rs.at[s, k - 1])
                consume(k - 1)

    def kv_part(h):
        loads[1, h].wait()
        loads[2, h].wait()
        run = None
        for c in range(groups):
            group = mm(blk(k_ref, c, h), blk(v_ref, c, h), 0, 0)
            if c > 0:
                loc[c, h] = run
            run = group if c == 0 else run + group
        k, at = spot(h)
        tot[0, k, at] = run

    def fwd_part(h):
        loads[0, h].wait()
        for c in range(groups):
            scores = mm(blk(q_ref, c, h), blk(k_ref, c, h), 1, 1)
            scores = jnp.where(causal, scores, 0.0).astype(BF16)
            fs[c, h] = scores
            att[c, h] = mm(scores, blk(v_ref, c, h), 1, 0)

    def guided(c, h):
        return gain_ref[:, h * HD:(h + 1) * HD] * blk(g_ref, c, h).astype(F32)

    def some(part_of, lo, hi):
        def go():
            for h in range(lo, hi):
                part_of(h)
        return go

    def each(part_of):
        def go(k):
            for h in range(k * TOGETHER, (k + 1) * TOGETHER):
                part_of(h)
        return go

    squares = [jnp.zeros((CH, HD), F32)] * groups
    crossed = [jnp.zeros((CH, HD), F32)] * groups

    def attend(h):
        if h == 0:
            gain_copy.wait()
        loads[3, h].wait()
        for c in range(groups):
            k, at = spot(h)
            state = cret[0, k, at]
            if c > 0:
                state = state + loc[c, h]
            state = state.astype(BF16)
            kvs[c, h] = state
            a = att[c, h] + mm(blk(q_ref, c, h), state, 1, 0)
            att[c, h] = a
            squares[c] = squares[c] + a * a
            crossed[c] = crossed[c] + guided(c, h) * a

    scan(0, False, each(kv_part), some(fwd_part, 0, heads // 2), some(fwd_part, heads // 2, heads), each(attend))

    for c in range(groups):
        zsrc[c:c + 1, :] = jnp.sum(squares[c].T, 0, keepdims=True)
        zsrc[groups + c:groups + c + 1, :] = jnp.sum(crossed[c].T, 0, keepdims=True)
    for d in far_first(nz):
        send(zsrc, zbuf.at[z], z_ss, z_rs, {"head": lax.rem(z + d, nz)})
    zbuf[z] = zsrc[...]
    arrived(zbuf.at[pl.ds(0, nz - 1)], z_rs)
    sums = zbuf[0]
    for j in range(1, nz):
        sums = sums + zbuf[j]
    sums = sums * (1.0 / width)
    inverse = lax.rsqrt(sums[:groups] + 1e-06)
    second = inverse * inverse * inverse * sums[groups:]
    inv = [jnp.broadcast_to(inverse[c:c + 1], (CH, CH)).T for c in range(groups)]
    sec = [jnp.broadcast_to(second[c:c + 1], (CH, CH)).T for c in range(groups)]

    def qd_part(h):
        run = None
        for c in range(groups - 1, -1, -1):
            grad = (inv[c] * guided(c, h) - sec[c] * att[c, h]).astype(BF16)
            ga[c, h] = grad
            group = mm(blk(q_ref, c, h), grad, 0, 0)
            if c < groups - 1:
                loc[c, h] = run
            run = group if c == groups - 1 else run + group
        k, at = spot(h)
        tot[1, k, at] = run

    def back_part(h):
        for c in range(groups):
            grad = ga[c, h]
            back = mm(grad, blk(v_ref, c, h), 1, 1)
            back = jnp.where(causal, back, 0.0).astype(BF16)
            gq = mm(back, blk(k_ref, c, h), 1, 0) + mm(grad, kvs[c, h], 1, 1)
            dq_ref[c * CH:(c + 1) * CH, h * HD:(h + 1) * HD] = gq.astype(BF16)
            att[c, h] = mm(back, blk(q_ref, c, h), 0, 0)
            gvp[c, h] = mm(fs[c, h], grad, 0, 0)
        store(0, dq_ref, dq_hbm, h)

    def finish(h):
        for c in range(groups):
            k, at = spot(h)
            state = cret[1, k, at]
            if c < groups - 1:
                state = state + loc[c, h]
            state = state.astype(BF16)
            gk = att[c, h] + mm(blk(v_ref, c, h), state, 1, 1)
            dk_ref[c * CH:(c + 1) * CH, h * HD:(h + 1) * HD] = gk.astype(BF16)
            gv = gvp[c, h] + mm(blk(k_ref, c, h), state, 1, 0)
            dv_ref[c * CH:(c + 1) * CH, h * HD:(h + 1) * HD] = gv.astype(BF16)
        store(1, dk_ref, dk_hbm, h)
        store(2, dv_ref, dv_hbm, h)

    scan(1, True, each(qd_part), some(back_part, 0, heads // 2), some(back_part, heads // 2, heads), each(finish))
    sent(0)
    sent(1)
    arrived(zbuf.at[pl.ds(0, nz - 1)], z_ss)
    for copy in stored:
        copy.wait()


def write_out(cuts, *refs):
    arrays = (len(refs) - 3) // 2
    held, in_s, out_s = refs[-3:]
    rows = refs[0].shape[0] // cuts
    pieces = [(n, i) for n in range(arrays) for i in range(cuts)]
    reads, writes = {}, []
    for n, i in pieces:
        at = pl.ds(i * rows, rows)
        reads[n, i] = pltpu.make_async_copy(refs[n].at[at], held.at[n, at], in_s.at[n, i])
        reads[n, i].start()
    for n, i in pieces:
        at = pl.ds(i * rows, rows)
        reads[n, i].wait()
        copy = pltpu.make_async_copy(held.at[n, at], refs[arrays + n].at[at], out_s.at[n, i])
        copy.start()
        writes.append(copy)
    for copy in writes:
        copy.wait()


def solution(mesh):
    ny = mesh.shape["seq"] // (2 * NX)
    nz = mesh.shape["head"]

    def on_device(query, key, value, upstream, gain):
        rows, columns = query.shape
        groups, heads = rows // CH, columns // HD
        half = TOGETHER * HD // 2
        part = half // NX
        chunks = heads // TOGETHER
        hbm = pl.BlockSpec(memory_space=pl.ANY)
        out = jax.ShapeDtypeStruct((rows, columns), BF16)
        dma = pltpu.SemaphoreType.DMA
        blocks = (groups, heads, CH, HD)
        whole = pltpu.VMEM((rows, columns), BF16)
        results = pl.pallas_call(
            functools.partial(kernel, ny, nz, columns * nz),
            name="linear_attention_backward",
            out_shape=(out, out, out),
            in_specs=[hbm] * 5,
            out_specs=(hbm, hbm, hbm),
            scratch_shapes=[
                whole, whole, whole,
                whole, whole, whole, whole, pltpu.VMEM((1, columns), F32),
                pltpu.VMEM(blocks, F32),
                pltpu.VMEM((2, chunks, 2 * half, HD), F32),
                pltpu.VMEM(blocks, BF16),
                pltpu.VMEM(blocks, F32),
                pltpu.VMEM(blocks, BF16),
                pltpu.VMEM(blocks, F32),
                pltpu.VMEM(blocks, BF16),
                pltpu.VMEM((2, chunks, half, HD), F32),
                pltpu.VMEM((2, chunks, half, HD), F32),
                pltpu.VMEM((2, chunks, NX, part, HD), F32),
                pltpu.VMEM((2, chunks, part, HD), F32),
                pltpu.VMEM((2, chunks, ny, part, HD), F32),
                pltpu.VMEM((2, chunks, NX, part, HD), F32),
                pltpu.VMEM((2, chunks, half, HD), F32),
                pltpu.VMEM((2, chunks, half, HD), F32),
                pltpu.VMEM((2, chunks, 2 * half, HD), F32),
                pltpu.VMEM((2 * groups, CH), F32),
                pltpu.VMEM((nz, 2 * groups, CH), F32),
                dma((3, heads)), dma((4, heads)), dma,
                dma((2,)), dma((2, chunks)),
                dma((2,)), dma((2, chunks)),
                dma((2,)), dma((2, chunks)),
                dma((2,)), dma((2, chunks)),
                dma((2,)), dma((2, chunks)),
                dma, dma,
            ],
            compiler_params=pltpu.CompilerParams(
                collective_id=0, has_side_effects=True, vmem_limit_bytes=61 * 1024 * 1024
            ),
        )(query, key, value, upstream, gain.reshape(1, columns))
        cuts = 4
        return pl.pallas_call(
            functools.partial(write_out, cuts),
            name="write_out",
            out_shape=(out, out, out),
            in_specs=[hbm] * 3,
            out_specs=(hbm, hbm, hbm),
            scratch_shapes=[
                pltpu.VMEM((3, rows, columns), BF16), dma((3, cuts)), dma((3, cuts)),
            ],
            compiler_params=pltpu.CompilerParams(vmem_limit_bytes=61 * 1024 * 1024),
        )(*results)

    spec = P("seq", "head")
    return jax.shard_map(
        on_device, mesh=mesh, in_specs=(spec, spec, spec, spec, P("head")),
        out_specs=(spec, spec, spec), check_vma=False,
    )
```

```python
import functools

import jax
import jax.numpy as jnp
from jax import lax
from jax.experimental import pallas as pl
from jax.experimental.pallas import tpu as pltpu
from jax.sharding import PartitionSpec as P

HD = 128
CH = 128
NX = 4
TOGETHER = 1
MESH = pl.DeviceIdType.MESH
F32 = jnp.float32
BF16 = jnp.bfloat16


def mm(a, b, ca, cb):
    return lax.dot_general(a, b, (((ca,), (cb,)), ((), ())), preferred_element_type=F32)


def far_first(n):
    return sorted(range(1, n), key=lambda d: -min(d, n - d))


def kernel(
    ny, nz, width,
    q_hbm, k_hbm, v_hbm, g_hbm, gain_hbm, dq_ref, dk_ref, dv_ref,
    q_ref, k_ref, v_ref, g_ref, gain_ref,
    loc, tot, fs, att, kvs, gvp, ga,
    xin, ysrc, ybuf, xret, cret, zsrc, zbuf,
    in_s, gain_s, x_ss, x_rs, y_ss, y_rs, r_ss, r_rs, z_ss, z_rs,
):
    groups = q_ref.shape[0] // CH
    heads = q_ref.shape[1] // HD
    chunks = heads // TOGETHER
    row_size = 2 * NX
    part = TOGETHER * HD // row_size
    me = lax.axis_index("seq")
    z = lax.axis_index("head")
    core = lax.rem(me, 2)
    x = lax.rem(me // 2, NX)
    y = me // row_size
    rank = lax.rem(me, row_size)
    hops = [(dx, dc) for dx in far_first(NX) for dc in (0, 1)] + [(0, 1)]
    row_peers = [lax.rem(x + dx, NX) * 2 + lax.rem(core + dc, 2) for dx, dc in hops]

    def load(n, src, dst, h):
        cols = slice(h * HD, (h + 1) * HD)
        copy = pltpu.make_async_copy(src.at[:, cols], dst.at[:, cols], in_s.at[n, h])
        copy.start()
        return copy

    loads = {}
    for h in range(heads):
        loads[1, h] = load(1, k_hbm, k_ref, h)
        loads[2, h] = load(2, v_hbm, v_ref, h)
    for h in range(heads):
        loads[0, h] = load(0, q_hbm, q_ref, h)
    for h in range(heads):
        loads[3, h] = load(3, g_hbm, g_ref, h)
    gain_copy = pltpu.make_async_copy(gain_hbm, gain_ref, gain_s)
    gain_copy.start()

    def in_row(j):
        return {"seq": y * row_size + j}

    def at_y(j):
        return {"seq": j * row_size + rank}

    ybuf[...] = jnp.zeros_like(ybuf)
    barrier = pltpu.get_barrier_semaphore()
    for d in range(1, ny):
        pl.semaphore_signal(barrier, inc=1, device_id=at_y(lax.rem(y + d, ny)), device_id_type=MESH)
    for d in range(1, nz):
        pl.semaphore_signal(barrier, inc=1, device_id={"head": lax.rem(z + d, nz)}, device_id_type=MESH)
    for j in row_peers:
        pl.semaphore_signal(barrier, inc=1, device_id=in_row(j), device_id_type=MESH)

    def send(src, dst, ss, rs, to):
        copy = pltpu.make_async_remote_copy(
            src_ref=src, dst_ref=dst, send_sem=ss, recv_sem=rs, device_id=to, device_id_type=MESH
        )
        copy.start()

    def blk(ref, c, h):
        return ref[c * CH:(c + 1) * CH, h * HD:(h + 1) * HD]

    row = lax.broadcasted_iota(jnp.int32, (CH, CH), 0)
    col = lax.broadcasted_iota(jnp.int32, (CH, CH), 1)
    causal = col <= row

    def share(j):
        return pl.ds(pl.multiple_of(j * part, part), part)

    def arrived(like, sem):
        pltpu.make_async_copy(like, like, sem).wait()

    def spot(h):
        return h // TOGETHER, slice(h % TOGETHER * HD, (h % TOGETHER + 1) * HD)

    def sent(s, reverse):
        arrived(xin.at[s, :, pl.ds(0, row_size - 1)], x_ss.at[s])
        for d in range(1, ny):
            to = y - d if reverse else y + d

            @pl.when(jnp.logical_and(to >= 0, to < ny))
            def _(d=d):
                arrived(ysrc.at[s], y_ss.at[s, d - 1])
        arrived(xret.at[s, :, pl.ds(0, row_size - 1)], r_ss.at[s])

    def scan(s, reverse, produce, beside_x, beside_y, consume):
        for k in range(chunks):
            produce(k)
            if s == 0 and k == 0:
                pl.semaphore_wait(barrier, (row_size - 1) + (ny - 1) + (nz - 1))
            for j in row_peers:
                send(tot.at[s, k, share(j)], xin.at[s, k, rank], x_ss.at[s], x_rs.at[s, k], in_row(j))
            xin[s, k, rank] = tot[s, k, share(rank)]
        beside_x()
        for k in range(chunks):
            arrived(xin.at[s, k, pl.ds(0, row_size - 1)], x_rs.at[s, k])
            total = xin[s, k, 0]
            for j in range(1, row_size):
                total = total + xin[s, k, j]
            ysrc[s, k] = total
            for d in far_first(ny):
                to = y - d if reverse else y + d

                @pl.when(jnp.logical_and(to >= 0, to < ny))
                def _(to=to, k=k, d=d):
                    send(
                        ysrc.at[s, k], ybuf.at[s, k, y],
                        y_ss.at[s, d - 1], y_rs.at[s, k, d - 1], at_y(to),
                    )
        beside_y()
        for k in range(chunks):
            for d in range(1, ny):
                source = y + d if reverse else y - d

                @pl.when(jnp.logical_and(source >= 0, source < ny))
                def _(k=k, d=d):
                    arrived(ysrc.at[s, k], y_rs.at[s, k, d - 1])
            run = ybuf[s, k, 0]
            for j in range(1, ny):
                run = run + ybuf[s, k, j]
            order = range(row_size - 1, -1, -1) if reverse else range(row_size)
            for j in order:
                xret[s, k, j] = run
                run = run + xin[s, k, j]
            for j in row_peers:
                send(xret.at[s, k, j], cret.at[s, k, share(rank)], r_ss.at[s], r_rs.at[s, k], in_row(j))
            cret[s, k, share(rank)] = xret[s, k, rank]
        for k in range(chunks):
            arrived(cret.at[s, k, pl.ds(0, (row_size - 1) * part)], r_rs.at[s, k])
            consume(k)

    def kv_part(h):
        loads[1, h].wait()
        loads[2, h].wait()
        run = None
        for c in range(groups):
            group = mm(blk(k_ref, c, h), blk(v_ref, c, h), 0, 0)
            if c > 0:
                loc[c, h] = run
            run = group if c == 0 else run + group
        k, at = spot(h)
        tot[0, k, at] = run

    def fwd_part(h):
        loads[0, h].wait()
        for c in range(groups):
            scores = mm(blk(q_ref, c, h), blk(k_ref, c, h), 1, 1)
            scores = jnp.where(causal, scores, 0.0).astype(BF16)
            fs[c, h] = scores
            att[c, h] = mm(scores, blk(v_ref, c, h), 1, 0)

    def guided(c, h):
        return gain_ref[:, h * HD:(h + 1) * HD] * blk(g_ref, c, h).astype(F32)

    def some(part_of, lo, hi):
        def go():
            for h in range(lo, hi):
                part_of(h)
        return go

    def each(part_of):
        def go(k):
            for h in range(k * TOGETHER, (k + 1) * TOGETHER):
                part_of(h)
        return go

    squares = [jnp.zeros((CH, HD), F32)] * groups
    crossed = [jnp.zeros((CH, HD), F32)] * groups

    def attend(h):
        if h == 0:
            gain_copy.wait()
        loads[3, h].wait()
        for c in range(groups):
            k, at = spot(h)
            state = cret[0, k, at]
            if c > 0:
                state = state + loc[c, h]
            state = state.astype(BF16)
            kvs[c, h] = state
            a = att[c, h] + mm(blk(q_ref, c, h), state, 1, 0)
            att[c, h] = a
            squares[c] = squares[c] + a * a
            crossed[c] = crossed[c] + guided(c, h) * a

    scan(0, False, each(kv_part), some(fwd_part, 0, heads // 2), some(fwd_part, heads // 2, heads), each(attend))

    for c in range(groups):
        zsrc[c:c + 1, :] = jnp.sum(squares[c].T, 0, keepdims=True)
        zsrc[groups + c:groups + c + 1, :] = jnp.sum(crossed[c].T, 0, keepdims=True)
    for d in far_first(nz):
        send(zsrc, zbuf.at[z], z_ss, z_rs, {"head": lax.rem(z + d, nz)})
    zbuf[z] = zsrc[...]
    arrived(zbuf.at[pl.ds(0, nz - 1)], z_rs)
    sums = zbuf[0]
    for j in range(1, nz):
        sums = sums + zbuf[j]
    sums = sums * (1.0 / width)
    inverse = lax.rsqrt(sums[:groups] + 1e-06)
    second = inverse * inverse * inverse * sums[groups:]
    inv = [jnp.broadcast_to(inverse[c:c + 1], (CH, CH)).T for c in range(groups)]
    sec = [jnp.broadcast_to(second[c:c + 1], (CH, CH)).T for c in range(groups)]

    def qd_part(h):
        run = None
        for c in range(groups - 1, -1, -1):
            grad = (inv[c] * guided(c, h) - sec[c] * att[c, h]).astype(BF16)
            ga[c, h] = grad
            group = mm(blk(q_ref, c, h), grad, 0, 0)
            if c < groups - 1:
                loc[c, h] = run
            run = group if c == groups - 1 else run + group
        k, at = spot(h)
        tot[1, k, at] = run

    def back_part(h):
        for c in range(groups):
            grad = ga[c, h]
            back = mm(grad, blk(v_ref, c, h), 1, 1)
            back = jnp.where(causal, back, 0.0).astype(BF16)
            gq = mm(back, blk(k_ref, c, h), 1, 0) + mm(grad, kvs[c, h], 1, 1)
            dq_ref[c * CH:(c + 1) * CH, h * HD:(h + 1) * HD] = gq.astype(BF16)
            att[c, h] = mm(back, blk(q_ref, c, h), 0, 0)
            gvp[c, h] = mm(fs[c, h], grad, 0, 0)

    def finish(h):
        for c in range(groups):
            k, at = spot(h)
            state = cret[1, k, at]
            if c < groups - 1:
                state = state + loc[c, h]
            state = state.astype(BF16)
            gk = att[c, h] + mm(blk(v_ref, c, h), state, 1, 1)
            dk_ref[c * CH:(c + 1) * CH, h * HD:(h + 1) * HD] = gk.astype(BF16)
            gv = gvp[c, h] + mm(blk(k_ref, c, h), state, 1, 0)
            dv_ref[c * CH:(c + 1) * CH, h * HD:(h + 1) * HD] = gv.astype(BF16)

    scan(1, True, each(qd_part), some(back_part, 0, heads // 2), some(back_part, heads // 2, heads), each(finish))
    sent(0, False)
    sent(1, True)
    arrived(zbuf.at[pl.ds(0, nz - 1)], z_ss)


def write_out(cuts, *refs):
    arrays = (len(refs) - 1) // 2
    sems = refs[-1]
    rows = refs[0].shape[0] // cuts
    writes = []
    for n in range(arrays):
        for i in range(cuts):
            at = pl.ds(i * rows, rows)
            writes.append(pltpu.make_async_copy(
                refs[n].at[at], refs[arrays + n].at[at], sems.at[n, i]
            ))
    for copy in writes:
        copy.start()
    for copy in writes:
        copy.wait()


def solution(mesh):
    ny = mesh.shape["seq"] // (2 * NX)
    nz = mesh.shape["head"]

    def on_device(query, key, value, upstream, gain):
        rows, columns = query.shape
        groups, heads = rows // CH, columns // HD
        row_size = 2 * NX
        part = TOGETHER * HD // row_size
        chunks = heads // TOGETHER
        vmem = pl.BlockSpec(memory_space=pltpu.VMEM)
        hbm = pl.BlockSpec(memory_space=pl.ANY)
        out = jax.ShapeDtypeStruct((rows, columns), BF16)
        dma = pltpu.SemaphoreType.DMA
        blocks = (groups, heads, CH, HD)
        whole = pltpu.VMEM((rows, columns), BF16)
        results = pl.pallas_call(
            functools.partial(kernel, ny, nz, columns * nz),
            name="linear_attention_backward",
            out_shape=(whole, whole, whole),
            in_specs=[hbm] * 5,
            out_specs=(vmem, vmem, vmem),
            scratch_shapes=[
                whole, whole, whole, whole, pltpu.VMEM((1, columns), F32),
                pltpu.VMEM(blocks, F32),
                pltpu.VMEM((2, chunks, TOGETHER * HD, HD), F32),
                pltpu.VMEM(blocks, BF16),
                pltpu.VMEM(blocks, F32),
                pltpu.VMEM(blocks, BF16),
                pltpu.VMEM(blocks, F32),
                pltpu.VMEM(blocks, BF16),
                pltpu.VMEM((2, chunks, row_size, part, HD), F32),
                pltpu.VMEM((2, chunks, part, HD), F32),
                pltpu.VMEM((2, chunks, ny, part, HD), F32),
                pltpu.VMEM((2, chunks, row_size, part, HD), F32),
                pltpu.VMEM((2, chunks, TOGETHER * HD, HD), F32),
                pltpu.VMEM((2 * groups, CH), F32),
                pltpu.VMEM((nz, 2 * groups, CH), F32),
                dma((4, heads)), dma,
                dma((2,)), dma((2, chunks)),
                dma((2, ny - 1)), dma((2, chunks, ny - 1)),
                dma((2,)), dma((2, chunks)),
                dma, dma,
            ],
            compiler_params=pltpu.CompilerParams(
                collective_id=0, has_side_effects=True, vmem_limit_bytes=61 * 1024 * 1024
            ),
        )(query, key, value, upstream, gain.reshape(1, columns))
        cuts = 4
        return pl.pallas_call(
            functools.partial(write_out, cuts),
            name="write_out",
            out_shape=(out, out, out),
            in_specs=[vmem] * 3,
            out_specs=(hbm, hbm, hbm),
            scratch_shapes=[dma((3, cuts))],
            compiler_params=pltpu.CompilerParams(vmem_limit_bytes=1024 * 1024),
        )(*results)

    spec = P("seq", "head")
    return jax.shard_map(
        on_device, mesh=mesh, in_specs=(spec, spec, spec, spec, P("head")),
        out_specs=(spec, spec, spec), check_vma=False,
    )
```

```python
import functools

import jax
import jax.numpy as jnp
from jax import lax
from jax.experimental import pallas as pl
from jax.experimental.pallas import tpu as pltpu
from jax.sharding import PartitionSpec as P

HD = 128
CH = 128
NX = 4
TOGETHER = 1
MESH = pl.DeviceIdType.MESH
F32 = jnp.float32
BF16 = jnp.bfloat16


def mm(a, b, ca, cb):
    return lax.dot_general(a, b, (((ca,), (cb,)), ((), ())), preferred_element_type=F32)


def far_first(n):
    return sorted(range(1, n), key=lambda d: -min(d, n - d))


def kernel(
    ny, nz, width,
    q_hbm, k_hbm, v_hbm, g_hbm, gain_hbm, dq_ref, dk_ref, dv_ref,
    q_ref, k_ref, v_ref, g_ref, gain_ref,
    loc, tot, fs, att, kvs, gvp, ga,
    xin, ysrc, ybuf, xret, cret, zsrc, zbuf,
    in_s, gain_s, x_ss, x_rs, y_ss, y_rs, r_ss, r_rs, z_ss, z_rs,
):
    groups = q_ref.shape[0] // CH
    heads = q_ref.shape[1] // HD
    chunks = heads // TOGETHER
    row_size = 2 * NX
    part = TOGETHER * HD // row_size
    me = lax.axis_index("seq")
    z = lax.axis_index("head")
    core = lax.rem(me, 2)
    x = lax.rem(me // 2, NX)
    y = me // row_size
    rank = lax.rem(me, row_size)
    hops = [(dx, dc) for dx in far_first(NX) for dc in (0, 1)] + [(0, 1)]
    row_peers = [lax.rem(x + dx, NX) * 2 + lax.rem(core + dc, 2) for dx, dc in hops]

    def load(n, src, dst, h):
        cols = slice(h * HD, (h + 1) * HD)
        copy = pltpu.make_async_copy(src.at[:, cols], dst.at[:, cols], in_s.at[n, h])
        copy.start()
        return copy

    def in_row(j):
        return {"seq": y * row_size + j}

    def at_y(j):
        return {"seq": j * row_size + rank}

    ybuf[...] = jnp.zeros_like(ybuf)
    barrier = pltpu.get_barrier_semaphore()
    for d in range(1, ny):
        pl.semaphore_signal(barrier, inc=1, device_id=at_y(lax.rem(y + d, ny)), device_id_type=MESH)
    for d in range(1, nz):
        pl.semaphore_signal(barrier, inc=1, device_id={"head": lax.rem(z + d, nz)}, device_id_type=MESH)
    for j in row_peers:
        pl.semaphore_signal(barrier, inc=1, device_id=in_row(j), device_id_type=MESH)

    def send(src, dst, ss, rs, to):
        copy = pltpu.make_async_remote_copy(
            src_ref=src, dst_ref=dst, send_sem=ss, recv_sem=rs, device_id=to, device_id_type=MESH
        )
        copy.start()

    loads = {}
    for h in range(heads):
        loads[1, h] = load(1, k_hbm, k_ref, h)
        loads[2, h] = load(2, v_hbm, v_ref, h)
    for h in range(heads):
        loads[0, h] = load(0, q_hbm, q_ref, h)
    for h in range(heads):
        loads[3, h] = load(3, g_hbm, g_ref, h)
    gain_copy = pltpu.make_async_copy(gain_hbm, gain_ref, gain_s)
    gain_copy.start()

    def blk(ref, c, h):
        return ref[c * CH:(c + 1) * CH, h * HD:(h + 1) * HD]

    row = lax.broadcasted_iota(jnp.int32, (CH, CH), 0)
    col = lax.broadcasted_iota(jnp.int32, (CH, CH), 1)
    causal = col <= row

    def share(j):
        return pl.ds(pl.multiple_of(j * part, part), part)

    def arrived(like, sem):
        pltpu.make_async_copy(like, like, sem).wait()

    def spot(h):
        return h // TOGETHER, slice(h % TOGETHER * HD, (h % TOGETHER + 1) * HD)

    def sent(s, reverse):
        arrived(xin.at[s, :, pl.ds(0, row_size - 1)], x_ss.at[s])
        for d in range(1, ny):
            to = y - d if reverse else y + d

            @pl.when(jnp.logical_and(to >= 0, to < ny))
            def _(d=d):
                arrived(ysrc.at[s], y_ss.at[s, d - 1])
        arrived(xret.at[s, :, pl.ds(0, row_size - 1)], r_ss.at[s])

    def scan(s, reverse, produce, beside_x, beside_y, consume):
        if s == 0:
            for k in range(chunks):
                produce(k)
            pl.semaphore_wait(barrier, (row_size - 1) + (ny - 1) + (nz - 1))
        for k in range(chunks):
            if s > 0:
                produce(k)
            for j in row_peers:
                send(tot.at[s, k, share(j)], xin.at[s, k, rank], x_ss.at[s], x_rs.at[s, k], in_row(j))
            xin[s, k, rank] = tot[s, k, share(rank)]
        beside_x()
        for k in range(chunks):
            arrived(xin.at[s, k, pl.ds(0, row_size - 1)], x_rs.at[s, k])
            total = xin[s, k, 0]
            for j in range(1, row_size):
                total = total + xin[s, k, j]
            ysrc[s, k] = total
            for d in range(ny - 1, 0, -1):
                to = y - d if reverse else y + d

                @pl.when(jnp.logical_and(to >= 0, to < ny))
                def _(to=to, k=k, d=d):
                    send(
                        ysrc.at[s, k], ybuf.at[s, k, y],
                        y_ss.at[s, d - 1], y_rs.at[s, k, d - 1], at_y(to),
                    )
        beside_y()
        for k in range(chunks):
            for d in range(1, ny):
                source = y + d if reverse else y - d

                @pl.when(jnp.logical_and(source >= 0, source < ny))
                def _(k=k, d=d):
                    arrived(ysrc.at[s, k], y_rs.at[s, k, d - 1])
            run = ybuf[s, k, 0]
            for j in range(1, ny):
                run = run + ybuf[s, k, j]
            order = range(row_size - 1, -1, -1) if reverse else range(row_size)
            for j in order:
                xret[s, k, j] = run
                run = run + xin[s, k, j]
            for j in row_peers:
                send(xret.at[s, k, j], cret.at[s, k, share(rank)], r_ss.at[s], r_rs.at[s, k], in_row(j))
            cret[s, k, share(rank)] = xret[s, k, rank]
        for k in range(chunks):
            arrived(cret.at[s, k, pl.ds(0, (row_size - 1) * part)], r_rs.at[s, k])
            consume(k)

    def kv_part(h):
        loads[1, h].wait()
        loads[2, h].wait()
        run = None
        for c in range(groups):
            group = mm(blk(k_ref, c, h), blk(v_ref, c, h), 0, 0)
            if c > 0:
                loc[c, h] = run
            run = group if c == 0 else run + group
        k, at = spot(h)
        tot[0, k, at] = run

    def fwd_part(h):
        loads[0, h].wait()
        for c in range(groups):
            scores = mm(blk(q_ref, c, h), blk(k_ref, c, h), 1, 1)
            scores = jnp.where(causal, scores, 0.0).astype(BF16)
            fs[c, h] = scores
            att[c, h] = mm(scores, blk(v_ref, c, h), 1, 0)

    def guided(c, h):
        return gain_ref[:, h * HD:(h + 1) * HD] * blk(g_ref, c, h).astype(F32)

    def some(part_of, lo, hi):
        def go():
            for h in range(lo, hi):
                part_of(h)
        return go

    def each(part_of):
        def go(k):
            for h in range(k * TOGETHER, (k + 1) * TOGETHER):
                part_of(h)
        return go

    squares = [jnp.zeros((CH, HD), F32)] * groups
    crossed = [jnp.zeros((CH, HD), F32)] * groups

    def attend(h):
        if h == 0:
            gain_copy.wait()
        loads[3, h].wait()
        for c in range(groups):
            k, at = spot(h)
            state = cret[0, k, at]
            if c > 0:
                state = state + loc[c, h]
            state = state.astype(BF16)
            kvs[c, h] = state
            a = att[c, h] + mm(blk(q_ref, c, h), state, 1, 0)
            att[c, h] = a
            squares[c] = squares[c] + a * a
            crossed[c] = crossed[c] + guided(c, h) * a

    scan(0, False, each(kv_part), some(fwd_part, 0, heads // 2), some(fwd_part, heads // 2, heads), each(attend))

    for c in range(groups):
        zsrc[c:c + 1, :] = jnp.sum(squares[c].T, 0, keepdims=True)
        zsrc[groups + c:groups + c + 1, :] = jnp.sum(crossed[c].T, 0, keepdims=True)
    for d in far_first(nz):
        send(zsrc, zbuf.at[z], z_ss, z_rs, {"head": lax.rem(z + d, nz)})
    zbuf[z] = zsrc[...]
    for h in range(heads):
        for c in range(groups):
            gvp[c, h] = guided(c, h)
    arrived(zbuf.at[pl.ds(0, nz - 1)], z_rs)
    sums = zbuf[0]
    for j in range(1, nz):
        sums = sums + zbuf[j]
    sums = sums * (1.0 / width)
    inverse = lax.rsqrt(sums[:groups] + 1e-06)
    second = inverse * inverse * inverse * sums[groups:]
    inv = [jnp.broadcast_to(inverse[c:c + 1], (CH, CH)).T for c in range(groups)]
    sec = [jnp.broadcast_to(second[c:c + 1], (CH, CH)).T for c in range(groups)]

    def qd_part(h):
        run = None
        for c in range(groups - 1, -1, -1):
            grad = (inv[c] * gvp[c, h] - sec[c] * att[c, h]).astype(BF16)
            ga[c, h] = grad
            group = mm(blk(q_ref, c, h), grad, 0, 0)
            if c < groups - 1:
                loc[c, h] = run
            run = group if c == groups - 1 else run + group
        k, at = spot(h)
        tot[1, k, at] = run

    def back_part(h):
        for c in range(groups):
            grad = ga[c, h]
            back = mm(grad, blk(v_ref, c, h), 1, 1)
            back = jnp.where(causal, back, 0.0).astype(BF16)
            gq = mm(back, blk(k_ref, c, h), 1, 0) + mm(grad, kvs[c, h], 1, 1)
            dq_ref[c * CH:(c + 1) * CH, h * HD:(h + 1) * HD] = gq.astype(BF16)
            att[c, h] = mm(back, blk(q_ref, c, h), 0, 0)
            gvp[c, h] = mm(fs[c, h], grad, 0, 0)

    def finish(h):
        for c in range(groups):
            k, at = spot(h)
            state = cret[1, k, at]
            if c < groups - 1:
                state = state + loc[c, h]
            state = state.astype(BF16)
            gk = att[c, h] + mm(blk(v_ref, c, h), state, 1, 1)
            dk_ref[c * CH:(c + 1) * CH, h * HD:(h + 1) * HD] = gk.astype(BF16)
            gv = gvp[c, h] + mm(blk(k_ref, c, h), state, 1, 0)
            dv_ref[c * CH:(c + 1) * CH, h * HD:(h + 1) * HD] = gv.astype(BF16)

    scan(1, True, each(qd_part), some(back_part, 0, heads // 2), some(back_part, heads // 2, heads), each(finish))
    sent(0, False)
    sent(1, True)
    arrived(zbuf.at[pl.ds(0, nz - 1)], z_ss)


def write_out(cuts, *refs):
    arrays = (len(refs) - 1) // 2
    sems = refs[-1]
    rows = refs[0].shape[0] // cuts
    writes = []
    for n in range(arrays):
        for i in range(cuts):
            at = pl.ds(i * rows, rows)
            writes.append(pltpu.make_async_copy(
                refs[n].at[at], refs[arrays + n].at[at], sems.at[n, i]
            ))
    for copy in writes:
        copy.start()
    for copy in writes:
        copy.wait()


def solution(mesh):
    ny = mesh.shape["seq"] // (2 * NX)
    nz = mesh.shape["head"]

    def on_device(query, key, value, upstream, gain):
        rows, columns = query.shape
        groups, heads = rows // CH, columns // HD
        row_size = 2 * NX
        part = TOGETHER * HD // row_size
        chunks = heads // TOGETHER
        vmem = pl.BlockSpec(memory_space=pltpu.VMEM)
        hbm = pl.BlockSpec(memory_space=pl.ANY)
        out = jax.ShapeDtypeStruct((rows, columns), BF16)
        dma = pltpu.SemaphoreType.DMA
        blocks = (groups, heads, CH, HD)
        whole = pltpu.VMEM((rows, columns), BF16)
        results = pl.pallas_call(
            functools.partial(kernel, ny, nz, columns * nz),
            name="linear_attention_backward",
            out_shape=(whole, whole, whole),
            in_specs=[hbm] * 5,
            out_specs=(vmem, vmem, vmem),
            scratch_shapes=[
                whole, whole, whole, whole, pltpu.VMEM((1, columns), F32),
                pltpu.VMEM(blocks, F32),
                pltpu.VMEM((2, chunks, TOGETHER * HD, HD), F32),
                pltpu.VMEM(blocks, BF16),
                pltpu.VMEM(blocks, F32),
                pltpu.VMEM(blocks, BF16),
                pltpu.VMEM(blocks, F32),
                pltpu.VMEM(blocks, BF16),
                pltpu.VMEM((2, chunks, row_size, part, HD), F32),
                pltpu.VMEM((2, chunks, part, HD), F32),
                pltpu.VMEM((2, chunks, ny, part, HD), F32),
                pltpu.VMEM((2, chunks, row_size, part, HD), F32),
                pltpu.VMEM((2, chunks, TOGETHER * HD, HD), F32),
                pltpu.VMEM((2 * groups, CH), F32),
                pltpu.VMEM((nz, 2 * groups, CH), F32),
                dma((4, heads)), dma,
                dma((2,)), dma((2, chunks)),
                dma((2, ny - 1)), dma((2, chunks, ny - 1)),
                dma((2,)), dma((2, chunks)),
                dma, dma,
            ],
            compiler_params=pltpu.CompilerParams(
                collective_id=0, has_side_effects=True, vmem_limit_bytes=61 * 1024 * 1024
            ),
        )(query, key, value, upstream, gain.reshape(1, columns))
        cuts = 1
        return pl.pallas_call(
            functools.partial(write_out, cuts),
            name="write_out",
            out_shape=(out, out, out),
            in_specs=[vmem] * 3,
            out_specs=(hbm, hbm, hbm),
            scratch_shapes=[dma((3, cuts))],
            compiler_params=pltpu.CompilerParams(vmem_limit_bytes=1024 * 1024),
        )(*results)

    spec = P("seq", "head")
    return jax.shard_map(
        on_device, mesh=mesh, in_specs=(spec, spec, spec, spec, P("head")),
        out_specs=(spec, spec, spec), check_vma=False,
    )
```

```python
import functools

import jax
import jax.numpy as jnp
from jax import lax
from jax.experimental import pallas as pl
from jax.experimental.pallas import tpu as pltpu
from jax.sharding import PartitionSpec as P

HD = 128
CH = 128
NX = 4
TOGETHER = 1
MESH = pl.DeviceIdType.MESH
F32 = jnp.float32
BF16 = jnp.bfloat16


def mm(a, b, ca, cb):
    return lax.dot_general(a, b, (((ca,), (cb,)), ((), ())), preferred_element_type=F32)


def far_first(n):
    return sorted(range(1, n), key=lambda d: -min(d, n - d))


def kernel(
    ny, nz, width,
    q_hbm, k_hbm, v_hbm, g_hbm, gain_hbm, dq_ref, dk_ref, dv_ref,
    q_ref, k_ref, v_ref, g_ref, gain_ref,
    loc, tot, fs, att, kvs, gvp, ga,
    xin, ysrc, ybuf, xret, cret, zsrc, zbuf,
    in_s, gain_s, x_ss, x_rs, y_ss, y_rs, r_ss, r_rs, z_ss, z_rs,
):
    groups = q_ref.shape[0] // CH
    heads = q_ref.shape[1] // HD
    chunks = heads // TOGETHER
    row_size = 2 * NX
    part = TOGETHER * HD // row_size
    me = lax.axis_index("seq")
    z = lax.axis_index("head")
    core = lax.rem(me, 2)
    x = lax.rem(me // 2, NX)
    y = me // row_size
    rank = lax.rem(me, row_size)
    hops = [(dx, dc) for dx in far_first(NX) for dc in (0, 1)] + [(0, 1)]
    row_peers = [lax.rem(x + dx, NX) * 2 + lax.rem(core + dc, 2) for dx, dc in hops]

    def load(n, src, dst, h):
        cols = slice(h * HD, (h + 1) * HD)
        copy = pltpu.make_async_copy(src.at[:, cols], dst.at[:, cols], in_s.at[n, h])
        copy.start()
        return copy

    def in_row(j):
        return {"seq": y * row_size + j}

    def at_y(j):
        return {"seq": j * row_size + rank}

    ybuf[...] = jnp.zeros_like(ybuf)
    barrier = pltpu.get_barrier_semaphore()
    for d in range(1, ny):
        pl.semaphore_signal(barrier, inc=1, device_id=at_y(lax.rem(y + d, ny)), device_id_type=MESH)
    for d in range(1, nz):
        pl.semaphore_signal(barrier, inc=1, device_id={"head": lax.rem(z + d, nz)}, device_id_type=MESH)
    for j in row_peers:
        pl.semaphore_signal(barrier, inc=1, device_id=in_row(j), device_id_type=MESH)

    def send(src, dst, ss, rs, to):
        copy = pltpu.make_async_remote_copy(
            src_ref=src, dst_ref=dst, send_sem=ss, recv_sem=rs, device_id=to, device_id_type=MESH
        )
        copy.start()

    loads = {}
    for h in range(heads):
        loads[1, h] = load(1, k_hbm, k_ref, h)
        loads[2, h] = load(2, v_hbm, v_ref, h)
    for h in range(heads):
        loads[0, h] = load(0, q_hbm, q_ref, h)
    for h in range(heads):
        loads[3, h] = load(3, g_hbm, g_ref, h)
    gain_copy = pltpu.make_async_copy(gain_hbm, gain_ref, gain_s)
    gain_copy.start()

    def blk(ref, c, h):
        return ref[c * CH:(c + 1) * CH, h * HD:(h + 1) * HD]

    row = lax.broadcasted_iota(jnp.int32, (CH, CH), 0)
    col = lax.broadcasted_iota(jnp.int32, (CH, CH), 1)
    causal = col <= row

    def share(j):
        return pl.ds(pl.multiple_of(j * part, part), part)

    def arrived(like, sem):
        pltpu.make_async_copy(like, like, sem).wait()

    def spot(h):
        return h // TOGETHER, slice(h % TOGETHER * HD, (h % TOGETHER + 1) * HD)

    def sent(s, reverse):
        arrived(xin.at[s, :, pl.ds(0, row_size - 1)], x_ss.at[s])
        for d in range(1, ny):
            to = y - d if reverse else y + d

            @pl.when(jnp.logical_and(to >= 0, to < ny))
            def _(d=d):
                arrived(ysrc.at[s], y_ss.at[s, d - 1])
        arrived(xret.at[s, :, pl.ds(0, row_size - 1)], r_ss.at[s])

    def scan(s, reverse, produce, beside_x, beside_y, consume):
        if s == 0:
            for k in range(chunks):
                produce(k)
            pl.semaphore_wait(barrier, (row_size - 1) + (ny - 1) + (nz - 1))
        for k in range(chunks):
            if s > 0:
                produce(k)
            for j in row_peers:
                send(tot.at[s, k, share(j)], xin.at[s, k, rank], x_ss.at[s], x_rs.at[s, k], in_row(j))
            xin[s, k, rank] = tot[s, k, share(rank)]
        beside_x()
        for k in range(chunks):
            arrived(xin.at[s, k, pl.ds(0, row_size - 1)], x_rs.at[s, k])
            total = xin[s, k, 0]
            for j in range(1, row_size):
                total = total + xin[s, k, j]
            ysrc[s, k] = total
            for d in range(ny - 1, 0, -1):
                to = y - d if reverse else y + d

                @pl.when(jnp.logical_and(to >= 0, to < ny))
                def _(to=to, k=k, d=d):
                    send(
                        ysrc.at[s, k], ybuf.at[s, k, y],
                        y_ss.at[s, d - 1], y_rs.at[s, k], at_y(to),
                    )
        beside_y()
        for k in range(chunks):
            for n in range(1, ny):

                @pl.when((ny - 1 - y if reverse else y) == n)
                def _(k=k, n=n):
                    arrived(ybuf.at[s, k, pl.ds(0, n)], y_rs.at[s, k])
            run = ybuf[s, k, 0]
            for j in range(1, ny):
                run = run + ybuf[s, k, j]
            order = range(row_size - 1, -1, -1) if reverse else range(row_size)
            for j in order:
                xret[s, k, j] = run
                run = run + xin[s, k, j]
            for j in row_peers:
                send(xret.at[s, k, j], cret.at[s, k, share(rank)], r_ss.at[s], r_rs.at[s, k], in_row(j))
            cret[s, k, share(rank)] = xret[s, k, rank]
        for k in range(chunks):
            arrived(cret.at[s, k, pl.ds(0, (row_size - 1) * part)], r_rs.at[s, k])
            consume(k)

    def kv_part(h):
        loads[1, h].wait()
        loads[2, h].wait()
        run = None
        for c in range(groups):
            group = mm(blk(k_ref, c, h), blk(v_ref, c, h), 0, 0)
            if c > 0:
                loc[c, h] = run
            run = group if c == 0 else run + group
        k, at = spot(h)
        tot[0, k, at] = run

    def fwd_part(h):
        loads[0, h].wait()
        for c in range(groups):
            scores = mm(blk(q_ref, c, h), blk(k_ref, c, h), 1, 1)
            scores = jnp.where(causal, scores, 0.0).astype(BF16)
            fs[c, h] = scores
            att[c, h] = mm(scores, blk(v_ref, c, h), 1, 0)

    def guided(c, h):
        return gain_ref[:, h * HD:(h + 1) * HD] * blk(g_ref, c, h).astype(F32)

    def some(part_of, lo, hi):
        def go():
            for h in range(lo, hi):
                part_of(h)
        return go

    def each(part_of):
        def go(k):
            for h in range(k * TOGETHER, (k + 1) * TOGETHER):
                part_of(h)
        return go

    squares = [jnp.zeros((CH, HD), F32)] * groups
    crossed = [jnp.zeros((CH, HD), F32)] * groups

    def attend(h):
        if h == 0:
            gain_copy.wait()
        loads[3, h].wait()
        for c in range(groups):
            k, at = spot(h)
            state = cret[0, k, at]
            if c > 0:
                state = state + loc[c, h]
            state = state.astype(BF16)
            kvs[c, h] = state
            a = att[c, h] + mm(blk(q_ref, c, h), state, 1, 0)
            att[c, h] = a
            squares[c] = squares[c] + a * a
            crossed[c] = crossed[c] + guided(c, h) * a

    scan(0, False, each(kv_part), some(fwd_part, 0, heads // 2), some(fwd_part, heads // 2, heads), each(attend))

    for c in range(groups):
        zsrc[c:c + 1, :] = jnp.sum(squares[c].T, 0, keepdims=True)
        zsrc[groups + c:groups + c + 1, :] = jnp.sum(crossed[c].T, 0, keepdims=True)
    for d in far_first(nz):
        send(zsrc, zbuf.at[z], z_ss, z_rs, {"head": lax.rem(z + d, nz)})
    zbuf[z] = zsrc[...]
    for h in range(heads):
        for c in range(groups):
            gvp[c, h] = guided(c, h)
    arrived(zbuf.at[pl.ds(0, nz - 1)], z_rs)
    sums = zbuf[0]
    for j in range(1, nz):
        sums = sums + zbuf[j]
    sums = sums * (1.0 / width)
    inverse = lax.rsqrt(sums[:groups] + 1e-06)
    second = inverse * inverse * inverse * sums[groups:]
    inv = [jnp.broadcast_to(inverse[c:c + 1], (CH, CH)).T for c in range(groups)]
    sec = [jnp.broadcast_to(second[c:c + 1], (CH, CH)).T for c in range(groups)]

    def qd_part(h):
        run = None
        for c in range(groups - 1, -1, -1):
            grad = (inv[c] * gvp[c, h] - sec[c] * att[c, h]).astype(BF16)
            ga[c, h] = grad
            group = mm(blk(q_ref, c, h), grad, 0, 0)
            if c < groups - 1:
                loc[c, h] = run
            run = group if c == groups - 1 else run + group
        k, at = spot(h)
        tot[1, k, at] = run

    def back_part(h):
        for c in range(groups):
            grad = ga[c, h]
            back = mm(grad, blk(v_ref, c, h), 1, 1)
            back = jnp.where(causal, back, 0.0).astype(BF16)
            gq = mm(back, blk(k_ref, c, h), 1, 0) + mm(grad, kvs[c, h], 1, 1)
            dq_ref[c * CH:(c + 1) * CH, h * HD:(h + 1) * HD] = gq.astype(BF16)
            att[c, h] = mm(back, blk(q_ref, c, h), 0, 0)
            gvp[c, h] = mm(fs[c, h], grad, 0, 0)

    def finish(h):
        for c in range(groups):
            k, at = spot(h)
            state = cret[1, k, at]
            if c < groups - 1:
                state = state + loc[c, h]
            state = state.astype(BF16)
            gk = att[c, h] + mm(blk(v_ref, c, h), state, 1, 1)
            dk_ref[c * CH:(c + 1) * CH, h * HD:(h + 1) * HD] = gk.astype(BF16)
            gv = gvp[c, h] + mm(blk(k_ref, c, h), state, 1, 0)
            dv_ref[c * CH:(c + 1) * CH, h * HD:(h + 1) * HD] = gv.astype(BF16)

    scan(1, True, each(qd_part), some(back_part, 0, heads // 2), some(back_part, heads // 2, heads), each(finish))
    sent(0, False)
    sent(1, True)
    arrived(zbuf.at[pl.ds(0, nz - 1)], z_ss)


def write_out(cuts, *refs):
    arrays = (len(refs) - 1) // 2
    sems = refs[-1]
    rows = refs[0].shape[0] // cuts
    writes = []
    for n in range(arrays):
        for i in range(cuts):
            at = pl.ds(i * rows, rows)
            writes.append(pltpu.make_async_copy(
                refs[n].at[at], refs[arrays + n].at[at], sems.at[n, i]
            ))
    for copy in writes:
        copy.start()
    for copy in writes:
        copy.wait()


def solution(mesh):
    ny = mesh.shape["seq"] // (2 * NX)
    nz = mesh.shape["head"]

    def on_device(query, key, value, upstream, gain):
        rows, columns = query.shape
        groups, heads = rows // CH, columns // HD
        row_size = 2 * NX
        part = TOGETHER * HD // row_size
        chunks = heads // TOGETHER
        vmem = pl.BlockSpec(memory_space=pltpu.VMEM)
        hbm = pl.BlockSpec(memory_space=pl.ANY)
        out = jax.ShapeDtypeStruct((rows, columns), BF16)
        dma = pltpu.SemaphoreType.DMA
        blocks = (groups, heads, CH, HD)
        whole = pltpu.VMEM((rows, columns), BF16)
        results = pl.pallas_call(
            functools.partial(kernel, ny, nz, columns * nz),
            name="linear_attention_backward",
            out_shape=(whole, whole, whole),
            in_specs=[hbm] * 5,
            out_specs=(vmem, vmem, vmem),
            scratch_shapes=[
                whole, whole, whole, whole, pltpu.VMEM((1, columns), F32),
                pltpu.VMEM(blocks, F32),
                pltpu.VMEM((2, chunks, TOGETHER * HD, HD), F32),
                pltpu.VMEM(blocks, BF16),
                pltpu.VMEM(blocks, F32),
                pltpu.VMEM(blocks, BF16),
                pltpu.VMEM(blocks, F32),
                pltpu.VMEM(blocks, BF16),
                pltpu.VMEM((2, chunks, row_size, part, HD), F32),
                pltpu.VMEM((2, chunks, part, HD), F32),
                pltpu.VMEM((2, chunks, ny, part, HD), F32),
                pltpu.VMEM((2, chunks, row_size, part, HD), F32),
                pltpu.VMEM((2, chunks, TOGETHER * HD, HD), F32),
                pltpu.VMEM((2 * groups, CH), F32),
                pltpu.VMEM((nz, 2 * groups, CH), F32),
                dma((4, heads)), dma,
                dma((2,)), dma((2, chunks)),
                dma((2, ny - 1)), dma((2, chunks)),
                dma((2,)), dma((2, chunks)),
                dma, dma,
            ],
            compiler_params=pltpu.CompilerParams(
                collective_id=0, has_side_effects=True, vmem_limit_bytes=61 * 1024 * 1024
            ),
        )(query, key, value, upstream, gain.reshape(1, columns))
        cuts = 1
        return pl.pallas_call(
            functools.partial(write_out, cuts),
            name="write_out",
            out_shape=(out, out, out),
            in_specs=[vmem] * 3,
            out_specs=(hbm, hbm, hbm),
            scratch_shapes=[dma((3, cuts))],
            compiler_params=pltpu.CompilerParams(vmem_limit_bytes=1024 * 1024),
        )(*results)

    spec = P("seq", "head")
    return jax.shard_map(
        on_device, mesh=mesh, in_specs=(spec, spec, spec, spec, P("head")),
        out_specs=(spec, spec, spec), check_vma=False,
    )
```
